32 devices in a mesh: gx: 2 (over y), gy: 4 (over z), gz: 4 (over x, core).
Axes of the slice: x: 2, y: 2, z: 4, core: 2. Of those that a mesh axis runs over, the one named last changes fastest.
Arguments:
- source: bfloat16 [8, 96, 2048], P('gx', 'gy', 'gz'), may hold values from -6 to 6
- tangent: bfloat16 [8, 96, 2048], P('gx', 'gy', 'gz'), may hold values from -6 to 6
- first_weight: bfloat16 [3, 3, 3, 64, 64], replicated, may hold values from -0.15625 to 0.15625
- first_bias: float32 [64], replicated, may hold values from -3 to 3
- second_weight: bfloat16 [3, 3, 3, 64, 64], replicated, may hold values from -0.15625 to 0.15625
- second_bias: float32 [64], replicated, may hold values from -3 to 3
Outputs:
- result: bfloat16 [8, 96, 2048], P('gx', 'gy', 'gz')
- result_tangent: bfloat16 [8, 96, 2048], P('gx', 'gy', 'gz')
The draws below stay inside these ranges and needn't reach their ends.
All inputs are finite; a program needn't handle non-finite values.
Results may differ from the reference program's by a relative error of at most 0.0052.
Values may be sent and summed in bfloat16 or wider, within the bound.
A program may use at most 64 MiB of HBM per device.

```python
import jax
import jax.numpy as jnp
from jax import lax

C = 64
NX = 8
NY = 96
NZ = 32


def level_of(rng, extent, shards, smallest, top_value):
    def one(dim, parts):
        draws = jax.random.uniform(jax.random.fold_in(jax.random.fold_in(rng, 6), dim), (parts,), jnp.float32, smallest / len(shards), top_value / len(shards))
        return jnp.repeat(jnp.exp(draws), extent[dim] // parts).reshape((-1,) + (1,) * (len(extent) - dim - 1))

    loudness = one(*shards[0])
    for cut in shards[1:]:
        loudness = loudness * one(*cut)
    return loudness


def bell_draw(key, extent, scale, most, pieces=(), kind=jnp.bfloat16):
    values = jax.random.normal(key, extent, jnp.float32) * scale
    if len(pieces) > 0:
        values = level_of(key, extent, pieces, -0.22, 0.18) * values
    return jnp.clip(values, min=-most, max=most).astype(kind)


def setup_inputs(seed: int = 0) -> dict:
    splits = jax.random.split(jax.random.key(seed), 7)
    return {
        "source": bell_draw(splits[0], (NX, NY, NZ * C), 1.0, 6.0, ((0, 2), (1, 4), (2, 4))),
        "tangent": bell_draw(splits[1], (NX, NY, NZ * C), 1.0, 6.0, ((0, 2), (1, 4), (2, 4))),
        "first_weight": bell_draw(splits[2], (3, 3, 3, C, C), (27 * C) ** -0.5, 0.15625),
        "first_bias": bell_draw(splits[3], (C,), 0.5, 3.0, (), jnp.float32),
        "second_weight": bell_draw(splits[4], (3, 3, 3, C, C), (27 * C) ** -0.5, 0.15625),
        "second_bias": bell_draw(splits[5], (C,), 0.5, 3.0, (), jnp.float32),
    }


def convolve(field, weight):
    return lax.conv_general_dilated(field, weight.astype(jnp.float32), (1, 1, 1), "SAME", dimension_numbers=("NDHWC", "DHWIO", "NDHWC"), precision=lax.Precision.HIGHEST)


def silu_slope(pre):
    sig = jax.nn.sigmoid(pre)
    return sig * (1.0 + pre * (1.0 - sig))


def reference(source, tangent, first_weight, first_bias, second_weight, second_bias):
    shape5 = (2, NX, NY, NZ, C)
    both = jnp.stack([source, tangent]).astype(jnp.float32).reshape(shape5)
    out1 = convolve(both, first_weight)
    pre1 = out1[0] + first_bias
    hidden = jax.nn.silu(pre1).astype(jnp.bfloat16)
    hidden_tangent = (silu_slope(pre1) * out1[1]).astype(jnp.bfloat16)
    both2 = jnp.stack([hidden, hidden_tangent]).astype(jnp.float32)
    out2 = convolve(both2, second_weight)
    pre2 = out2[0] + second_bias
    result = jax.nn.silu(pre2).astype(jnp.bfloat16).reshape(NX, NY, NZ * C)
    result_tangent = (silu_slope(pre2) * out2[1]).astype(jnp.bfloat16).reshape(NX, NY, NZ * C)
    return result, result_tangent
```

```python
import functools

import jax
import jax.numpy as jnp
from jax import lax
from jax.experimental import pallas as pl
from jax.experimental.pallas import tpu as pltpu
from jax.sharding import PartitionSpec as P

MESH = pl.DeviceIdType.MESH
F32 = jnp.float32
BF16 = jnp.bfloat16
ROWS = 32
PLANE = [(dy, dz) for dy in (-1, 0, 1) for dz in (-1, 0, 1) if dy or dz]
X_MSG = {(s, f): 2 * s + f for s in range(2) for f in range(2)}
A_Z = {(s, f): 4 + 2 * s + f for s in range(2) for f in range(2)}
A_S = {(s, z): 8 + 3 * s + z for s in range(2) for z in range(3)}
B_Z = {(s, k): 14 + 2 * s + k for s in range(2) for k in range(2)}
B_S = {(s, z): 18 + 3 * s + z for s in range(2) for z in range(3)}
MESSAGES = 24
STEP = (-1, 1)


def band_store(band, weight):
    zero64 = jnp.zeros((64, 64), BF16)
    zero128 = jnp.zeros((128, 128), BF16)
    for dx in range(3):
        for dy in range(3):
            taps = weight[dx, dy].reshape(192, 64)
            pair = jnp.concatenate(
                [
                    jnp.concatenate([taps, zero64], axis=0),
                    jnp.concatenate([zero64, taps], axis=0),
                ],
                axis=1,
            )
            r, c = dx * 384, dy * 256
            band[r : r + 256, c : c + 128] = pair
            band[r + 256 : r + 384, c : c + 128] = zero128
            band[r : r + 128, c + 128 : c + 256] = zero128
            band[r + 128 : r + 384, c + 128 : c + 256] = pair


def pack_strips(field, strips):
    row = lax.broadcasted_iota(jnp.int32, (8, 512), 0)
    low, high = [], []
    for f in range(2):
        first = jnp.zeros((8, 512), F32)
        last = jnp.zeros((8, 512), F32)
        for x in range(4):
            here = (row // 2) == x
            top = field[f, x, 0:8, :].astype(F32)
            end = field[f, x, 16:24, :].astype(F32)
            if x:
                top = pltpu.roll(top, 2 * x, 0)
            if x != 3:
                end = pltpu.roll(end, 2 + 2 * x, 0)
            first = jnp.where(here, top, first)
            last = jnp.where(here, end, last)
        low.append(first)
        high.append(last)
    strips[0] = jnp.concatenate(low, axis=0).astype(BF16)
    strips[1] = jnp.concatenate(high, axis=0).astype(BF16)


def assemble(grid, places, field, z_halo, strips):
    row = lax.broadcasted_iota(jnp.int32, (8, 768), 0)
    for f in range(2):
        above = strips[1].astype(F32)[8 * f : 8 * f + 8]
        below = strips[0].astype(F32)[8 * f : 8 * f + 8]
        for x in range(4):
            place = places[x]
            grid[f, place, 0:24, 0:128] = z_halo[1, f, x]
            grid[f, place, 0:24, 128:640] = field[f, x]
            grid[f, place, 0:24, 640:768] = z_halo[0, f, x]
            down = pltpu.roll(below, (8 - 2 * x) % 8, 0) if x else below
            up = pltpu.roll(above, 6 - 2 * x, 0) if x != 3 else above
            edge = jnp.where(row < 2, down, jnp.where(row >= 6, up, 0.0))
            grid[f, place, 24:32, :] = edge.astype(BF16)


def taps_sum(part, count, lanes):
    part = part.reshape(2 * count, ROWS, 3 * lanes)
    return (
        pltpu.roll(part[:, :, 0:lanes], 1, 1)
        + part[:, :, lanes : 2 * lanes]
        + pltpu.roll(part[:, :, 2 * lanes : 3 * lanes], ROWS - 1, 1)
    ).reshape(2, count, ROWS, lanes)


def conv_wide(grid, band, first, count, lane):
    rows = [
        grid[:, first + dx : first + dx + count, :, lane : lane + 384].reshape(
            2 * count * ROWS, 384
        )
        for dx in range(3)
    ]
    part = jnp.dot(
        jnp.concatenate(rows, axis=1), band[...], preferred_element_type=F32
    )
    return taps_sum(part, count, 256)


def conv_narrow(grid, band, first, count, lane):
    rows = [
        grid[:, first + dx : first + dx + count, :, lane : lane + 256].reshape(
            2 * count * ROWS, 256
        )
        for dx in range(3)
    ]
    weights = jnp.concatenate(
        [
            jnp.concatenate(
                [band[dx * 384 : dx * 384 + 256, dy * 256 : dy * 256 + 128] for dy in range(3)],
                axis=1,
            )
            for dx in range(3)
        ],
        axis=0,
    )
    part = jnp.dot(jnp.concatenate(rows, axis=1), weights, preferred_element_type=F32)
    return taps_sum(part, count, 128)


def silu_pair(total, bias):
    pre = total[0] + bias
    sig = jax.nn.sigmoid(pre)
    return pre * sig, sig * (1.0 + pre * (1.0 - sig)) * total[1]


def kernel(
    nx,
    ny,
    nz,
    source,
    tangent,
    w_one,
    b_one,
    w_two,
    b_two,
    out,
    out_tangent,
    own,
    x_halo,
    z_halo,
    strip_send,
    strip_halo,
    weights,
    bands,
    grid,
    hidden,
    local_sem,
    send_sem,
    recv_sem,
):
    ix, iy, iz = lax.axis_index("gx"), lax.axis_index("gy"), lax.axis_index("gz")

    def has(dx, dy, dz):
        ok = None
        for i, n, d in ((ix, nx, dx), (iy, ny, dy), (iz, nz, dz)):
            if d:
                this = (i > 0) if d < 0 else (i < n - 1)
                ok = this if ok is None else ok & this
        return ok

    inputs = (source, tangent)
    loads = [
        pltpu.make_async_copy(source, own.at[0], local_sem.at[0]),
        pltpu.make_async_copy(tangent, own.at[1], local_sem.at[1]),
        pltpu.make_async_copy(w_one, weights.at[0], local_sem.at[2]),
        pltpu.make_async_copy(w_two, weights.at[1], local_sem.at[3]),
    ]
    for load in loads:
        load.start()

    barrier = pltpu.get_barrier_semaphore()
    around = [(d, 0, 0) for d in STEP] + [(0, dy, dz) for dy, dz in PLANE]
    for d in around:

        @pl.when(has(*d))
        def _(d=d):
            pl.semaphore_signal(
                barrier, inc=1, device_id=(ix + d[0], iy + d[1], iz + d[2]), device_id_type=MESH
            )

    def remote(src, dst, index, d):
        return pltpu.make_async_remote_copy(
            src_ref=src,
            dst_ref=dst,
            send_sem=send_sem.at[index],
            recv_sem=recv_sem.at[index],
            device_id=(ix + d[0], iy + d[1], iz + d[2]),
            device_id_type=MESH,
        )

    def lanes_of(s):
        return pl.ds(0, 128) if s == 0 else pl.ds(384, 128)

    def x_copy(s, f):
        src = inputs[f].at[pl.ds(0, 2)] if s == 0 else inputs[f].at[pl.ds(2, 2)]
        dst = x_halo.at[f, pl.ds(2, 2)] if s == 0 else x_halo.at[f, pl.ds(0, 2)]
        d = (STEP[s], 0, 0)
        return remote(src, dst, X_MSG[s, f], d), has(*d), has(-d[0], 0, 0)

    def a_z_copy(s, f):
        d = (0, 0, STEP[s])
        src = inputs[f].at[:, :, lanes_of(s)]
        return remote(src, z_halo.at[0, s, f], A_Z[s, f], d), has(*d), has(0, 0, -d[2])

    def b_z_copy(s, k):
        d = (0, 0, STEP[s])
        src = x_halo.at[:, pl.ds(2 * k, 2), :, lanes_of(s)]
        dst = z_halo.at[1, s, :, pl.ds(2 * k, 2)]
        there = has(STEP[k], 0, 0)
        return remote(src, dst, B_Z[s, k], d), has(*d) & there, has(0, 0, -d[2]) & there

    def strip_copy(phase, s, z):
        d = (0, STEP[s], z - 1)
        src = strip_send.at[phase, s]
        if z == 0:
            src, dst = src.at[:, pl.ds(0, 128)], pl.ds(640, 128)
        elif z == 1:
            dst = pl.ds(128, 512)
        else:
            src, dst = src.at[:, pl.ds(384, 128)], pl.ds(0, 128)
        index = (A_S, B_S)[phase][s, z]
        return (
            remote(src, strip_halo.at[phase, s, :, dst], index, d),
            has(*d),
            has(0, -d[1], -d[2]),
        )

    x_copies = [x_copy(s, f) for s in range(2) for f in range(2)]
    a_copies = [a_z_copy(s, f) for s in range(2) for f in range(2)]
    a_strips = [strip_copy(0, s, z) for s in range(2) for z in range(3)]
    b_copies = [b_z_copy(s, k) for s in range(2) for k in range(2)]
    b_strips = [strip_copy(1, s, z) for s in range(2) for z in range(3)]

    def start(copies):
        for copy, send, _ in copies:
            pl.when(send)(copy.start)

    def wait_recv(copies):
        for copy, _, come in copies:
            pl.when(come)(copy.wait_recv)

    def wait_send(copies):
        for copy, send, _ in copies:
            pl.when(send)(copy.wait_send)

    arrivals = sum(has(*d).astype(jnp.int32) for d in around)
    pl.semaphore_wait(barrier, arrivals)
    start(x_copies)
    start(a_copies)

    loads[0].wait()
    loads[1].wait()
    pack_strips(own, strip_send.at[0])
    start(a_strips)

    for s in range(2):
        @pl.when(jnp.logical_not(has(STEP[s], 0, 0)))
        def _(s=s):
            x_halo[:, 2 * s : 2 * s + 2] = jnp.zeros((2, 2, 24, 512), BF16)
            for z in range(2):
                z_halo[1, z, :, 2 * s : 2 * s + 2] = jnp.zeros((2, 2, 24, 128), BF16)

        @pl.when(jnp.logical_not(has(0, 0, -STEP[s])))
        def _(s=s):
            z_halo[0, s] = jnp.zeros((2, 4, 24, 128), BF16)
            for k in range(2):

                @pl.when(has(STEP[k], 0, 0))
                def _():
                    z_halo[1, s, :, 2 * k : 2 * k + 2] = jnp.zeros((2, 2, 24, 128), BF16)

        for z, (lane, size) in enumerate(((640, 128), (128, 512), (0, 128))):

            @pl.when(jnp.logical_not(has(0, -STEP[s], 1 - z)))
            def _(s=s, lane=lane, size=size):
                for phase in range(2):
                    strip_halo[phase, s, :, lane : lane + size] = jnp.zeros((16, size), BF16)

    loads[2].wait()
    band_store(bands.at[0], weights.at[0])

    wait_recv(x_copies)
    pack_strips(x_halo, strip_send.at[1])
    start(b_copies)
    start(b_strips)

    loads[3].wait()
    band_store(bands.at[1], weights.at[1])

    wait_recv(a_copies)
    wait_recv(a_strips)
    assemble(grid, (2, 3, 4, 5), own, z_halo.at[0], strip_halo.at[0])

    bias_one = jnp.concatenate([b_one[...]] * 4, axis=1)
    bias_two = jnp.concatenate([b_two[...]] * 4, axis=1)

    def first_layer(begin, count):
        row = lax.broadcasted_iota(jnp.int32, (count, ROWS, 256), 1)
        lane = lax.broadcasted_iota(jnp.int32, (count, ROWS, 256), 2)
        layer = lax.broadcasted_iota(jnp.int32, (count, ROWS, 256), 0) + begin
        inside = (row < 24) | ((row == 24) & (iy < ny - 1)) | ((row == 31) & (iy > 0))
        inside &= (layer > 0) | (ix > 0)
        inside &= (layer < 5) | (ix < nx - 1)
        for block in range(3):
            size = 128 if block == 2 else 256
            conv = conv_narrow if block == 2 else conv_wide
            total = conv(grid, bands.at[0], begin, count, block * 256)
            value, slope = silu_pair(total, bias_one[:, :size])
            keep = inside[:, :, :size]
            if block == 0:
                keep &= (lane >= 64) | (iz > 0)
            if block == 2:
                keep &= (lane[:, :, :size] < 64) | (iz < nz - 1)
            for f, part in enumerate((value, slope)):
                hidden[f, begin : begin + count, :, block * 256 : block * 256 + size] = jnp.where(
                    keep, part, 0.0
                ).astype(BF16)

    first_layer(2, 2)

    wait_recv(b_copies)
    wait_recv(b_strips)
    assemble(grid, (0, 1, 6, 7), x_halo, z_halo.at[1], strip_halo.at[1])
    first_layer(0, 2)
    first_layer(4, 2)

    for block in range(2):
        total = conv_wide(hidden, bands.at[1], 0, 4, block * 256)
        value, slope = silu_pair(total, bias_two)
        cols = pl.ds(block * 256, 256)
        out[:, :, cols] = value[:, 0:24].astype(BF16)
        out_tangent[:, :, cols] = slope[:, 0:24].astype(BF16)

    wait_send(x_copies)
    wait_send(a_copies)
    wait_send(a_strips)
    wait_send(b_copies)
    wait_send(b_strips)


def solution(mesh):
    nx, ny, nz = mesh.shape["gx"], mesh.shape["gy"], mesh.shape["gz"]

    def shards(source, tangent, w_one, b_one, w_two, b_two):
        assert source.shape == (4, 24, 512)
        anywhere = pl.BlockSpec(memory_space=pl.ANY)
        vmem = pl.BlockSpec(memory_space=pltpu.VMEM)
        shape = jax.ShapeDtypeStruct(source.shape, source.dtype)
        return pl.pallas_call(
            functools.partial(kernel, nx, ny, nz),
            out_shape=(shape, shape),
            in_specs=[anywhere, anywhere, anywhere, vmem, anywhere, vmem],
            out_specs=(vmem, vmem),
            scratch_shapes=[
                pltpu.VMEM((2, 4, 24, 512), BF16),
                pltpu.VMEM((2, 4, 24, 512), BF16),
                pltpu.VMEM((2, 2, 2, 4, 24, 128), BF16),
                pltpu.VMEM((2, 2, 16, 512), BF16),
                pltpu.VMEM((2, 2, 16, 768), BF16),
                pltpu.VMEM((2, 3, 3, 3, 64, 64), BF16),
                pltpu.VMEM((2, 1152, 768), BF16),
                pltpu.VMEM((2, 8, ROWS, 768), BF16),
                pltpu.VMEM((2, 6, ROWS, 640), BF16),
                pltpu.SemaphoreType.DMA((4,)),
                pltpu.SemaphoreType.DMA((MESSAGES,)),
                pltpu.SemaphoreType.DMA((MESSAGES,)),
            ],
            compiler_params=pltpu.CompilerParams(
                collective_id=0, has_side_effects=True, vmem_limit_bytes=40 * 1024 * 1024
            ),
        )(source, tangent, w_one, b_one.reshape(1, 64), w_two, b_two.reshape(1, 64))

    return jax.shard_map(
        shards,
        mesh=mesh,
        in_specs=(P("gx", "gy", "gz"), P("gx", "gy", "gz"), P(), P(), P(), P()),
        out_specs=(P("gx", "gy", "gz"), P("gx", "gy", "gz")),
        check_vma=False,
    )
```

```python
import functools

import jax
import jax.numpy as jnp
from jax import lax
from jax.experimental import pallas as pl
from jax.experimental.pallas import tpu as pltpu
from jax.sharding import PartitionSpec as P

MESH = pl.DeviceIdType.MESH
F32 = jnp.float32
BF16 = jnp.bfloat16
ROWS = 32
AROUND = [
    (dx, dy, dz) for dx in (-1, 0, 1) for dy in (-1, 0, 1) for dz in (-1, 0, 1) if dx or dy or dz
]
STEP = (-1, 1)


def band_store(band, weight):
    zero64 = jnp.zeros((64, 64), BF16)
    zero128 = jnp.zeros((128, 128), BF16)
    for dx in range(3):
        for dy in range(3):
            taps = weight[dx, dy].reshape(192, 64)
            pair = jnp.concatenate(
                [
                    jnp.concatenate([taps, zero64], axis=0),
                    jnp.concatenate([zero64, taps], axis=0),
                ],
                axis=1,
            )
            r, c = dx * 384, dy * 256
            band[r : r + 256, c : c + 128] = pair
            band[r + 256 : r + 384, c : c + 128] = zero128
            band[r : r + 128, c + 128 : c + 256] = zero128
            band[r + 128 : r + 384, c + 128 : c + 256] = pair


def pack_strips(field, strips):
    row = lax.broadcasted_iota(jnp.int32, (8, 512), 0)
    low, high = [], []
    for f in range(2):
        first = jnp.zeros((8, 512), F32)
        last = jnp.zeros((8, 512), F32)
        for x in range(4):
            here = (row // 2) == x
            top = field[f, x, 0:8, :].astype(F32)
            end = field[f, x, 16:24, :].astype(F32)
            if x:
                top = pltpu.roll(top, 2 * x, 0)
            if x != 3:
                end = pltpu.roll(end, 2 + 2 * x, 0)
            first = jnp.where(here, top, first)
            last = jnp.where(here, end, last)
        low.append(first)
        high.append(last)
    strips[0] = jnp.concatenate(low, axis=0).astype(BF16)
    strips[1] = jnp.concatenate(high, axis=0).astype(BF16)


def assemble(grid, places, field, z_halo, strips, packed):
    row = lax.broadcasted_iota(jnp.int32, (8, 768), 0)
    for f in range(2):
        for x in range(4):
            place = places[x]
            grid[f, place, 0:24, 0:128] = z_halo[1, f, x]
            grid[f, place, 0:24, 128:640] = field[f, x]
            grid[f, place, 0:24, 640:768] = z_halo[0, f, x]
            at = packed[x]
            down = strips[x][0].astype(F32)[8 * f : 8 * f + 8]
            up = strips[x][1].astype(F32)[8 * f : 8 * f + 8]
            down = pltpu.roll(down, 8 - 2 * at, 0) if at else down
            up = pltpu.roll(up, 6 - 2 * at, 0) if at != 3 else up
            edge = jnp.where(row < 2, down, jnp.where(row >= 6, up, 0.0))
            grid[f, place, 24:32, :] = edge.astype(BF16)


def taps_sum(part, count, lanes):
    part = part.reshape(2 * count, ROWS, 3 * lanes)
    return (
        pltpu.roll(part[:, :, 0:lanes], 1, 1)
        + part[:, :, lanes : 2 * lanes]
        + pltpu.roll(part[:, :, 2 * lanes : 3 * lanes], ROWS - 1, 1)
    ).reshape(2, count, ROWS, lanes)


def conv_wide(grid, band, first, count, lane):
    rows = [
        grid[:, first + dx : first + dx + count, :, lane : lane + 384].reshape(
            2 * count * ROWS, 384
        )
        for dx in range(3)
    ]
    part = jnp.dot(
        jnp.concatenate(rows, axis=1), band[...], preferred_element_type=F32
    )
    return taps_sum(part, count, 256)


def conv_narrow(grid, band, first, count, lane):
    rows = [
        grid[:, first + dx : first + dx + count, :, lane : lane + 256].reshape(
            2 * count * ROWS, 256
        )
        for dx in range(3)
    ]
    weights = jnp.concatenate(
        [
            jnp.concatenate(
                [band[dx * 384 : dx * 384 + 256, dy * 256 : dy * 256 + 128] for dy in range(3)],
                axis=1,
            )
            for dx in range(3)
        ],
        axis=0,
    )
    part = jnp.dot(jnp.concatenate(rows, axis=1), weights, preferred_element_type=F32)
    return taps_sum(part, count, 128)


def silu_pair(total, bias):
    pre = total[0] + bias
    sig = jax.nn.sigmoid(pre)
    return pre * sig, sig * (1.0 + pre * (1.0 - sig)) * total[1]


def kernel(
    nx,
    ny,
    nz,
    source,
    tangent,
    w_one,
    b_one,
    w_two,
    b_two,
    out,
    out_tangent,
    own,
    x_halo,
    z_halo,
    strip_send,
    strip_halo,
    weights,
    biases,
    bands,
    grid,
    hidden,
    local_sem,
    send_sem,
    recv_sem,
):
    ix, iy, iz = lax.axis_index("gx"), lax.axis_index("gy"), lax.axis_index("gz")

    def has(dx, dy, dz):
        ok = None
        for i, n, d in ((ix, nx, dx), (iy, ny, dy), (iz, nz, dz)):
            if d:
                this = (i > 0) if d < 0 else (i < n - 1)
                ok = this if ok is None else ok & this
        return ok

    loads = [
        pltpu.make_async_copy(source, own.at[0], local_sem.at[0]),
        pltpu.make_async_copy(tangent, own.at[1], local_sem.at[1]),
        pltpu.make_async_copy(w_one, weights.at[0], local_sem.at[2]),
        pltpu.make_async_copy(w_two, weights.at[1], local_sem.at[3]),
        pltpu.make_async_copy(b_one, biases.at[0], local_sem.at[4]),
        pltpu.make_async_copy(b_two, biases.at[1], local_sem.at[5]),
    ]
    for load in loads:
        load.start()

    barrier = pltpu.get_barrier_semaphore()
    for d in AROUND:

        @pl.when(has(*d))
        def _(d=d):
            pl.semaphore_signal(
                barrier, inc=1, device_id=(ix + d[0], iy + d[1], iz + d[2]), device_id_type=MESH
            )

    def remote(src, dst, index, d):
        return pltpu.make_async_remote_copy(
            src_ref=src,
            dst_ref=dst,
            send_sem=send_sem.at[index],
            recv_sem=recv_sem.at[index],
            device_id=(ix + d[0], iy + d[1], iz + d[2]),
            device_id_type=MESH,
        )

    def lanes_of(s):
        return pl.ds(0, 128) if s == 0 else pl.ds(384, 128)

    def copy_to(d):
        dx, dy, dz = d
        if dy == 0:
            slot = pl.ds(0, 4) if dx == 0 else pl.ds(0 if dx > 0 else 2, 2)
            layers = pl.ds(0, 4) if dx == 0 else pl.ds(2 if dx > 0 else 0, 2)
            if dz == 0:
                src, dst = own.at[:, layers], x_halo.at[:, slot]
            else:
                src = own.at[:, layers, :, lanes_of(dz > 0)]
                dst = z_halo.at[int(dx != 0), int(dz > 0), :, slot]
        else:
            src = strip_send.at[int(dy > 0)]
            if dz == 0:
                dst = pl.ds(128, 512)
            else:
                src = src.at[:, lanes_of(dz > 0)]
                dst = pl.ds(0 if dz > 0 else 640, 128)
            dst = strip_halo.at[dx + 1, int(dy > 0), :, dst]
        return remote(src, dst, AROUND.index(d), d), has(*d), has(-dx, -dy, -dz)

    def group(depth, strip):
        return [copy_to(d) for d in AROUND if (d[0] != 0) == depth and (d[1] != 0) == strip]

    x_copies, x_strips = group(True, False), group(True, True)
    a_copies, a_strips = group(False, False), group(False, True)

    def start(copies):
        for copy, send, _ in copies:
            pl.when(send)(copy.start)

    def wait_recv(copies):
        for copy, _, come in copies:
            pl.when(come)(copy.wait_recv)

    def wait_send(copies):
        for copy, send, _ in copies:
            pl.when(send)(copy.wait_send)

    arrivals = sum(has(*d).astype(jnp.int32) for d in AROUND)
    pl.semaphore_wait(barrier, arrivals)
    loads[0].wait()
    loads[1].wait()
    start(x_copies)
    start(a_copies)

    pack_strips(own, strip_send)
    start(x_strips)
    start(a_strips)

    for s in range(2):
        @pl.when(jnp.logical_not(has(STEP[s], 0, 0)))
        def _(s=s):
            x_halo[:, 2 * s : 2 * s + 2] = jnp.zeros((2, 2, 24, 512), BF16)
            for z in range(2):
                z_halo[1, z, :, 2 * s : 2 * s + 2] = jnp.zeros((2, 2, 24, 128), BF16)
                strip_halo[2 - 2 * s, z] = jnp.zeros((16, 768), BF16)

        @pl.when(jnp.logical_not(has(0, 0, -STEP[s])))
        def _(s=s):
            z_halo[0, s] = jnp.zeros((2, 4, 24, 128), BF16)
            for k in range(2):

                @pl.when(has(STEP[k], 0, 0))
                def _():
                    z_halo[1, s, :, 2 * k : 2 * k + 2] = jnp.zeros((2, 2, 24, 128), BF16)

        for z, (lane, size) in enumerate(((640, 128), (128, 512), (0, 128))):

            @pl.when(jnp.logical_not(has(0, -STEP[s], 1 - z)))
            def _(s=s, lane=lane, size=size):
                for side in range(3):
                    strip_halo[side, s, :, lane : lane + size] = jnp.zeros((16, size), BF16)

    loads[2].wait()
    band_store(bands.at[0], weights.at[0])

    loads[3].wait()
    band_store(bands.at[1], weights.at[1])

    wait_recv(a_copies)
    wait_recv(a_strips)
    assemble(grid, (2, 3, 4, 5), own, z_halo.at[0], (strip_halo.at[1],) * 4, range(4))

    loads[4].wait()
    loads[5].wait()
    bias_one = jnp.concatenate([biases[0]] * 4, axis=1)
    bias_two = jnp.concatenate([biases[1]] * 4, axis=1)

    def first_layer(begin, count):
        row = lax.broadcasted_iota(jnp.int32, (count, ROWS, 256), 1)
        lane = lax.broadcasted_iota(jnp.int32, (count, ROWS, 256), 2)
        layer = lax.broadcasted_iota(jnp.int32, (count, ROWS, 256), 0) + begin
        inside = (row < 24) | ((row == 24) & (iy < ny - 1)) | ((row == 31) & (iy > 0))
        inside &= (layer > 0) | (ix > 0)
        inside &= (layer < 5) | (ix < nx - 1)
        for block in range(3):
            size = 128 if block == 2 else 256
            conv = conv_narrow if block == 2 else conv_wide
            total = conv(grid, bands.at[0], begin, count, block * 256)
            value, slope = silu_pair(total, bias_one[:, :size])
            keep = inside[:, :, :size]
            if block == 0:
                keep &= (lane >= 64) | (iz > 0)
            if block == 2:
                keep &= (lane[:, :, :size] < 64) | (iz < nz - 1)
            for f, part in enumerate((value, slope)):
                hidden[f, begin : begin + count, :, block * 256 : block * 256 + size] = jnp.where(
                    keep, part, 0.0
                ).astype(BF16)

    first_layer(2, 2)

    wait_recv(x_copies)
    wait_recv(x_strips)
    assemble(grid, (0, 1, 6, 7), x_halo, z_halo.at[1], (strip_halo.at[2],) * 2 + (strip_halo.at[0],) * 2, (2, 3, 0, 1))
    first_layer(0, 2)
    first_layer(4, 2)

    for block in range(2):
        total = conv_wide(hidden, bands.at[1], 0, 4, block * 256)
        value, slope = silu_pair(total, bias_two)
        cols = pl.ds(block * 256, 256)
        out[:, :, cols] = value[:, 0:24].astype(BF16)
        out_tangent[:, :, cols] = slope[:, 0:24].astype(BF16)

    wait_send(x_copies)
    wait_send(a_copies)
    wait_send(a_strips)
    wait_send(x_strips)


def solution(mesh):
    nx, ny, nz = mesh.shape["gx"], mesh.shape["gy"], mesh.shape["gz"]

    def shards(source, tangent, w_one, b_one, w_two, b_two):
        assert source.shape == (4, 24, 512)
        hbm = pl.BlockSpec(memory_space=pltpu.HBM)
        vmem = pl.BlockSpec(memory_space=pltpu.VMEM)
        shape = jax.ShapeDtypeStruct(source.shape, source.dtype)
        return pl.pallas_call(
            functools.partial(kernel, nx, ny, nz),
            out_shape=(shape, shape),
            in_specs=[hbm] * 6,
            out_specs=(vmem, vmem),
            scratch_shapes=[
                pltpu.VMEM((2, 4, 24, 512), BF16),
                pltpu.VMEM((2, 4, 24, 512), BF16),
                pltpu.VMEM((2, 2, 2, 4, 24, 128), BF16),
                pltpu.VMEM((2, 16, 512), BF16),
                pltpu.VMEM((3, 2, 16, 768), BF16),
                pltpu.VMEM((2, 3, 3, 3, 64, 64), BF16),
                pltpu.VMEM((2, 1, 64), F32),
                pltpu.VMEM((2, 1152, 768), BF16),
                pltpu.VMEM((2, 8, ROWS, 768), BF16),
                pltpu.VMEM((2, 6, ROWS, 640), BF16),
                pltpu.SemaphoreType.DMA((6,)),
                pltpu.SemaphoreType.DMA((len(AROUND),)),
                pltpu.SemaphoreType.DMA((len(AROUND),)),
            ],
            compiler_params=pltpu.CompilerParams(
                collective_id=0, has_side_effects=True, vmem_limit_bytes=64 * 1024 * 1024
            ),
        )(source, tangent, w_one, b_one.reshape(1, 64), w_two, b_two.reshape(1, 64))
    return jax.shard_map(
        shards,
        mesh=mesh,
        in_specs=(P("gx", "gy", "gz"), P("gx", "gy", "gz"), P(), P(), P(), P()),
        out_specs=(P("gx", "gy", "gz"), P("gx", "gy", "gz")),
        check_vma=False,
    )
```

```python
import functools

import jax
import jax.numpy as jnp
from jax import lax
from jax.experimental import pallas as pl
from jax.experimental.pallas import tpu as pltpu
from jax.sharding import PartitionSpec as P

MESH = pl.DeviceIdType.MESH
F32 = jnp.float32
BF16 = jnp.bfloat16
ROWS = 32
AROUND = [
    (dx, dy, dz) for dx in (-1, 0, 1) for dy in (-1, 0, 1) for dz in (-1, 0, 1) if dx or dy or dz
]
STEP = (-1, 1)


def band_store(band, weight):
    zero64 = jnp.zeros((64, 64), BF16)
    zero128 = jnp.zeros((128, 128), BF16)
    for dx in range(3):
        for dy in range(3):
            taps = weight[dx, dy].reshape(192, 64)
            pair = jnp.concatenate(
                [
                    jnp.concatenate([taps, zero64], axis=0),
                    jnp.concatenate([zero64, taps], axis=0),
                ],
                axis=1,
            )
            r, c = dx * 384, dy * 256
            band[r : r + 256, c : c + 128] = pair
            band[r + 256 : r + 384, c : c + 128] = zero128
            band[r : r + 128, c + 128 : c + 256] = zero128
            band[r + 128 : r + 384, c + 128 : c + 256] = pair


def pack_strips(field, strips):
    row = lax.broadcasted_iota(jnp.int32, (8, 512), 0)
    low, high = [], []
    for f in range(2):
        first = jnp.zeros((8, 512), F32)
        last = jnp.zeros((8, 512), F32)
        for x in range(4):
            here = (row // 2) == x
            top = field[f, x, 0:8, :].astype(F32)
            end = field[f, x, 16:24, :].astype(F32)
            if x:
                top = pltpu.roll(top, 2 * x, 0)
            if x != 3:
                end = pltpu.roll(end, 2 + 2 * x, 0)
            first = jnp.where(here, top, first)
            last = jnp.where(here, end, last)
        low.append(first)
        high.append(last)
    strips[0] = jnp.concatenate(low, axis=0).astype(BF16)
    strips[1] = jnp.concatenate(high, axis=0).astype(BF16)


def assemble(grid, places, field, z_halo, strips, packed):
    row = lax.broadcasted_iota(jnp.int32, (8, 768), 0)
    for f in range(2):
        for x in range(4):
            place = places[x]
            grid[f, place, 0:24, 0:128] = z_halo[1, f, x]
            grid[f, place, 0:24, 128:640] = field[f, x]
            grid[f, place, 0:24, 640:768] = z_halo[0, f, x]
            at = packed[x]
            down = strips[x][0].astype(F32)[8 * f : 8 * f + 8]
            up = strips[x][1].astype(F32)[8 * f : 8 * f + 8]
            down = pltpu.roll(down, 8 - 2 * at, 0) if at else down
            up = pltpu.roll(up, 6 - 2 * at, 0) if at != 3 else up
            edge = jnp.where(row < 2, down, jnp.where(row >= 6, up, 0.0))
            grid[f, place, 24:32, :] = edge.astype(BF16)


def taps_sum(part, count, lanes):
    part = part.reshape(2 * count, ROWS, 3 * lanes)
    return (
        pltpu.roll(part[:, :, 0:lanes], 1, 1)
        + part[:, :, lanes : 2 * lanes]
        + pltpu.roll(part[:, :, 2 * lanes : 3 * lanes], ROWS - 1, 1)
    ).reshape(2, count, ROWS, lanes)


def conv_wide(grid, band, first, count, lane):
    rows = [
        grid[:, first + dx : first + dx + count, :, lane : lane + 384].reshape(
            2 * count * ROWS, 384
        )
        for dx in range(3)
    ]
    part = jnp.dot(
        jnp.concatenate(rows, axis=1), band[...], preferred_element_type=F32
    )
    return taps_sum(part, count, 256)


def conv_narrow(grid, band, first, count, lane):
    rows = [
        grid[:, first + dx : first + dx + count, :, lane : lane + 256].reshape(
            2 * count * ROWS, 256
        )
        for dx in range(3)
    ]
    weights = jnp.concatenate(
        [
            jnp.concatenate(
                [band[dx * 384 : dx * 384 + 256, dy * 256 : dy * 256 + 128] for dy in range(3)],
                axis=1,
            )
            for dx in range(3)
        ],
        axis=0,
    )
    part = jnp.dot(jnp.concatenate(rows, axis=1), weights, preferred_element_type=F32)
    return taps_sum(part, count, 128)


def silu_pair(total, bias):
    pre = total[0] + bias
    sig = jax.nn.sigmoid(pre)
    return pre * sig, sig * (1.0 + pre * (1.0 - sig)) * total[1]


def kernel(
    nx,
    ny,
    nz,
    source,
    tangent,
    w_one,
    b_one,
    w_two,
    b_two,
    out,
    out_tangent,
    own,
    x_halo,
    z_halo,
    strip_send,
    strip_halo,
    weights,
    biases,
    bands,
    grid,
    hidden,
    local_sem,
    send_sem,
    recv_sem,
):
    ix, iy, iz = lax.axis_index("gx"), lax.axis_index("gy"), lax.axis_index("gz")

    def has(dx, dy, dz):
        ok = None
        for i, n, d in ((ix, nx, dx), (iy, ny, dy), (iz, nz, dz)):
            if d:
                this = (i > 0) if d < 0 else (i < n - 1)
                ok = this if ok is None else ok & this
        return ok

    loads = [
        pltpu.make_async_copy(source, own.at[0], local_sem.at[0]),
        pltpu.make_async_copy(tangent, own.at[1], local_sem.at[1]),
        pltpu.make_async_copy(w_one, weights.at[0], local_sem.at[2]),
        pltpu.make_async_copy(w_two, weights.at[1], local_sem.at[3]),
        pltpu.make_async_copy(b_one, biases.at[0], local_sem.at[4]),
        pltpu.make_async_copy(b_two, biases.at[1], local_sem.at[5]),
    ]
    for load in loads:
        load.start()

    barrier = pltpu.get_barrier_semaphore()
    for d in AROUND:

        @pl.when(has(*d))
        def _(d=d):
            pl.semaphore_signal(
                barrier, inc=1, device_id=(ix + d[0], iy + d[1], iz + d[2]), device_id_type=MESH
            )

    def remote(src, dst, index, d):
        return pltpu.make_async_remote_copy(
            src_ref=src,
            dst_ref=dst,
            send_sem=send_sem.at[index],
            recv_sem=recv_sem.at[index],
            device_id=(ix + d[0], iy + d[1], iz + d[2]),
            device_id_type=MESH,
        )

    def lanes_of(s):
        return pl.ds(0, 128) if s == 0 else pl.ds(384, 128)

    def copy_to(d):
        dx, dy, dz = d
        if dy == 0:
            slot = pl.ds(0, 4) if dx == 0 else pl.ds(0 if dx > 0 else 2, 2)
            layers = pl.ds(0, 4) if dx == 0 else pl.ds(2 if dx > 0 else 0, 2)
            if dz == 0:
                src, dst = own.at[:, layers], x_halo.at[:, slot]
            else:
                src = own.at[:, layers, :, lanes_of(dz > 0)]
                dst = z_halo.at[int(dx != 0), int(dz > 0), :, slot]
        else:
            src = strip_send.at[int(dy > 0)]
            if dz == 0:
                dst = pl.ds(128, 512)
            else:
                src = src.at[:, lanes_of(dz > 0)]
                dst = pl.ds(0 if dz > 0 else 640, 128)
            dst = strip_halo.at[dx + 1, int(dy > 0), :, dst]
        return remote(src, dst, AROUND.index(d), d), has(*d), has(-dx, -dy, -dz)

    def group(depth, strip):
        return [copy_to(d) for d in AROUND if (d[0] != 0) == depth and (d[1] != 0) == strip]

    x_copies, x_strips = group(True, False), group(True, True)
    a_copies, a_strips = group(False, False), group(False, True)

    def start(copies):
        for copy, send, _ in copies:
            pl.when(send)(copy.start)

    def wait_recv(copies):
        for copy, _, come in copies:
            pl.when(come)(copy.wait_recv)

    def wait_send(copies):
        for copy, send, _ in copies:
            pl.when(send)(copy.wait_send)

    arrivals = sum(has(*d).astype(jnp.int32) for d in AROUND)
    pl.semaphore_wait(barrier, arrivals)
    loads[0].wait()
    loads[1].wait()
    start(x_copies)
    start(a_copies)

    pack_strips(own, strip_send)
    start(x_strips)
    start(a_strips)

    for s in range(2):
        @pl.when(jnp.logical_not(has(STEP[s], 0, 0)))
        def _(s=s):
            x_halo[:, 2 * s : 2 * s + 2] = jnp.zeros((2, 2, 24, 512), BF16)
            for z in range(2):
                z_halo[1, z, :, 2 * s : 2 * s + 2] = jnp.zeros((2, 2, 24, 128), BF16)
                strip_halo[2 - 2 * s, z] = jnp.zeros((16, 768), BF16)

        @pl.when(jnp.logical_not(has(0, 0, -STEP[s])))
        def _(s=s):
            z_halo[0, s] = jnp.zeros((2, 4, 24, 128), BF16)
            for k in range(2):

                @pl.when(has(STEP[k], 0, 0))
                def _():
                    z_halo[1, s, :, 2 * k : 2 * k + 2] = jnp.zeros((2, 2, 24, 128), BF16)

        for z, (lane, size) in enumerate(((640, 128), (128, 512), (0, 128))):

            @pl.when(jnp.logical_not(has(0, -STEP[s], 1 - z)))
            def _(s=s, lane=lane, size=size):
                for side in range(3):
                    strip_halo[side, s, :, lane : lane + size] = jnp.zeros((16, size), BF16)

    loads[2].wait()
    band_store(bands.at[0], weights.at[0])

    loads[3].wait()
    band_store(bands.at[1], weights.at[1])

    wait_recv(a_copies)
    wait_recv(a_strips)
    assemble(grid, (2, 3, 4, 5), own, z_halo.at[0], (strip_halo.at[1],) * 4, range(4))

    loads[4].wait()
    loads[5].wait()
    bias_one = jnp.concatenate([biases[0]] * 4, axis=1)
    bias_two = jnp.concatenate([biases[1]] * 4, axis=1)

    def first_layer(begin, count):
        row = lax.broadcasted_iota(jnp.int32, (count, ROWS, 256), 1)
        lane = lax.broadcasted_iota(jnp.int32, (count, ROWS, 256), 2)
        layer = lax.broadcasted_iota(jnp.int32, (count, ROWS, 256), 0) + begin
        inside = (row < 24) | ((row == 24) & (iy < ny - 1)) | ((row == 31) & (iy > 0))
        inside &= (layer > 0) | (ix > 0)
        inside &= (layer < 5) | (ix < nx - 1)
        for block in range(3):
            size = 128 if block == 2 else 256
            conv = conv_narrow if block == 2 else conv_wide
            total = conv(grid, bands.at[0], begin, count, block * 256)
            value, slope = silu_pair(total, bias_one[:, :size])
            keep = inside[:, :, :size]
            if block == 0:
                keep &= (lane >= 64) | (iz > 0)
            if block == 2:
                keep &= (lane[:, :, :size] < 64) | (iz < nz - 1)
            for f, part in enumerate((value, slope)):
                hidden[f, begin : begin + count, :, block * 256 : block * 256 + size] = jnp.where(
                    keep, part, 0.0
                ).astype(BF16)

    first_layer(2, 2)

    wait_recv(x_copies)
    wait_recv(x_strips)
    assemble(grid, (0, 1, 6, 7), x_halo, z_halo.at[1], (strip_halo.at[2],) * 2 + (strip_halo.at[0],) * 2, (2, 3, 0, 1))
    first_layer(0, 2)
    first_layer(4, 2)

    for block in range(2):
        total = conv_wide(hidden, bands.at[1], 0, 4, block * 256)
        value, slope = silu_pair(total, bias_two)
        cols = pl.ds(block * 256, 256)
        out[:, :, cols] = value[:, 0:24].astype(BF16)
        out_tangent[:, :, cols] = slope[:, 0:24].astype(BF16)

    wait_send(x_copies)
    wait_send(a_copies)
    wait_send(a_strips)
    wait_send(x_strips)


def solution(mesh):
    nx, ny, nz = mesh.shape["gx"], mesh.shape["gy"], mesh.shape["gz"]

    def shards(source, tangent, w_one, b_one, w_two, b_two):
        assert source.shape == (4, 24, 512)
        hbm = pl.BlockSpec(memory_space=pltpu.HBM)
        vmem = pl.BlockSpec(memory_space=pltpu.VMEM)
        shape = pltpu.VMEM(source.shape, source.dtype)
        return pl.pallas_call(
            functools.partial(kernel, nx, ny, nz),
            out_shape=(shape, shape),
            in_specs=[hbm] * 6,
            out_specs=(vmem, vmem),
            scratch_shapes=[
                pltpu.VMEM((2, 4, 24, 512), BF16),
                pltpu.VMEM((2, 4, 24, 512), BF16),
                pltpu.VMEM((2, 2, 2, 4, 24, 128), BF16),
                pltpu.VMEM((2, 16, 512), BF16),
                pltpu.VMEM((3, 2, 16, 768), BF16),
                pltpu.VMEM((2, 3, 3, 3, 64, 64), BF16),
                pltpu.VMEM((2, 1, 64), F32),
                pltpu.VMEM((2, 1152, 768), BF16),
                pltpu.VMEM((2, 8, ROWS, 768), BF16),
                pltpu.VMEM((2, 6, ROWS, 640), BF16),
                pltpu.SemaphoreType.DMA((6,)),
                pltpu.SemaphoreType.DMA((len(AROUND),)),
                pltpu.SemaphoreType.DMA((len(AROUND),)),
            ],
            compiler_params=pltpu.CompilerParams(
                collective_id=0, has_side_effects=True, vmem_limit_bytes=62 * 1024 * 1024
            ),
        )(source, tangent, w_one, b_one.reshape(1, 64), w_two, b_two.reshape(1, 64))
    return jax.shard_map(
        shards,
        mesh=mesh,
        in_specs=(P("gx", "gy", "gz"), P("gx", "gy", "gz"), P(), P(), P(), P()),
        out_specs=(P("gx", "gy", "gz"), P("gx", "gy", "gz")),
        check_vma=False,
    )
```

```python
import functools

import jax
import jax.numpy as jnp
from jax import lax
from jax.experimental import pallas as pl
from jax.experimental.pallas import tpu as pltpu
from jax.sharding import PartitionSpec as P

MESH = pl.DeviceIdType.MESH
F32 = jnp.float32
BF16 = jnp.bfloat16
ROWS = 32
AROUND = [
    (dx, dy, dz) for dx in (-1, 0, 1) for dy in (-1, 0, 1) for dz in (-1, 0, 1) if dx or dy or dz
]
STEP = (-1, 1)


def band_store(band, weight):
    zero64 = jnp.zeros((64, 64), BF16)
    zero128 = jnp.zeros((128, 128), BF16)
    for dx in range(3):
        for dy in range(3):
            taps = weight[dx, dy].reshape(192, 64)
            pair = jnp.concatenate(
                [
                    jnp.concatenate([taps, zero64], axis=0),
                    jnp.concatenate([zero64, taps], axis=0),
                ],
                axis=1,
            )
            r, c = dx * 384, dy * 256
            band[r : r + 256, c : c + 128] = pair
            band[r + 256 : r + 384, c : c + 128] = zero128
            band[r : r + 128, c + 128 : c + 256] = zero128
            band[r + 128 : r + 384, c + 128 : c + 256] = pair


def pack_strips(field, strips):
    row = lax.broadcasted_iota(jnp.int32, (8, 512), 0)
    low, high = [], []
    for f in range(2):
        first = jnp.zeros((8, 512), F32)
        last = jnp.zeros((8, 512), F32)
        for x in range(4):
            here = (row // 2) == x
            top = field[f, x, 0:8, :].astype(F32)
            end = field[f, x, 16:24, :].astype(F32)
            if x:
                top = pltpu.roll(top, 2 * x, 0)
            if x != 3:
                end = pltpu.roll(end, 2 + 2 * x, 0)
            first = jnp.where(here, top, first)
            last = jnp.where(here, end, last)
        low.append(first)
        high.append(last)
    strips[0] = jnp.concatenate(low, axis=0).astype(BF16)
    strips[1] = jnp.concatenate(high, axis=0).astype(BF16)


def assemble(grid, places, field, z_halo, strips, packed):
    row = lax.broadcasted_iota(jnp.int32, (8, 768), 0)
    for f in range(2):
        for x in range(4):
            place = places[x]
            grid[f, place, 0:24, 0:128] = z_halo[1, f, x]
            grid[f, place, 0:24, 128:640] = field[f, x]
            grid[f, place, 0:24, 640:768] = z_halo[0, f, x]
            at = packed[x]
            down = strips[x][0].astype(F32)[8 * f : 8 * f + 8]
            up = strips[x][1].astype(F32)[8 * f : 8 * f + 8]
            down = pltpu.roll(down, 8 - 2 * at, 0) if at else down
            up = pltpu.roll(up, 6 - 2 * at, 0) if at != 3 else up
            edge = jnp.where(row < 2, down, jnp.where(row >= 6, up, 0.0))
            grid[f, place, 24:32, :] = edge.astype(BF16)


def taps_sum(part, count, lanes):
    part = part.reshape(2 * count, ROWS, 3 * lanes)
    return (
        pltpu.roll(part[:, :, 0:lanes], 1, 1)
        + part[:, :, lanes : 2 * lanes]
        + pltpu.roll(part[:, :, 2 * lanes : 3 * lanes], ROWS - 1, 1)
    ).reshape(2, count, ROWS, lanes)


def conv_wide(grid, band, first, count, lane):
    rows = [
        grid[:, first + dx : first + dx + count, :, lane : lane + 384].reshape(
            2 * count * ROWS, 384
        )
        for dx in range(3)
    ]
    part = jnp.dot(
        jnp.concatenate(rows, axis=1), band[...], preferred_element_type=F32
    )
    return taps_sum(part, count, 256)


def conv_narrow(grid, band, first, count, lane):
    rows = [
        grid[:, first + dx : first + dx + count, :, lane : lane + 256].reshape(
            2 * count * ROWS, 256
        )
        for dx in range(3)
    ]
    weights = jnp.concatenate(
        [
            jnp.concatenate(
                [band[dx * 384 : dx * 384 + 256, dy * 256 : dy * 256 + 128] for dy in range(3)],
                axis=1,
            )
            for dx in range(3)
        ],
        axis=0,
    )
    part = jnp.dot(jnp.concatenate(rows, axis=1), weights, preferred_element_type=F32)
    return taps_sum(part, count, 128)


def silu_pair(total, bias):
    pre = total[0] + bias
    sig = jax.nn.sigmoid(pre)
    return pre * sig, sig * (1.0 + pre * (1.0 - sig)) * total[1]


def kernel(
    nx,
    ny,
    nz,
    source,
    tangent,
    w_one,
    b_one,
    w_two,
    b_two,
    out,
    out_tangent,
    own,
    x_halo,
    z_halo,
    strip_send,
    strip_halo,
    weights,
    biases,
    bands,
    grid,
    hidden,
    local_sem,
    send_sem,
    recv_sem,
):
    ix, iy, iz = lax.axis_index("gx"), lax.axis_index("gy"), lax.axis_index("gz")

    def has(dx, dy, dz):
        ok = None
        for i, n, d in ((ix, nx, dx), (iy, ny, dy), (iz, nz, dz)):
            if d:
                this = (i > 0) if d < 0 else (i < n - 1)
                ok = this if ok is None else ok & this
        return ok

    loads = [
        pltpu.make_async_copy(source, own.at[0], local_sem.at[0]),
        pltpu.make_async_copy(tangent, own.at[1], local_sem.at[1]),
        pltpu.make_async_copy(w_one, weights.at[0], local_sem.at[2]),
        pltpu.make_async_copy(w_two, weights.at[1], local_sem.at[3]),
        pltpu.make_async_copy(b_one, biases.at[0], local_sem.at[4]),
        pltpu.make_async_copy(b_two, biases.at[1], local_sem.at[5]),
    ]
    for load in loads:
        load.start()

    barrier = pltpu.get_barrier_semaphore()
    for d in AROUND:

        @pl.when(has(*d))
        def _(d=d):
            pl.semaphore_signal(
                barrier, inc=1, device_id=(ix + d[0], iy + d[1], iz + d[2]), device_id_type=MESH
            )

    def remote(src, dst, index, d):
        return pltpu.make_async_remote_copy(
            src_ref=src,
            dst_ref=dst,
            send_sem=send_sem.at[index],
            recv_sem=recv_sem.at[index],
            device_id=(ix + d[0], iy + d[1], iz + d[2]),
            device_id_type=MESH,
        )

    def lanes_of(s):
        return pl.ds(0, 128) if s == 0 else pl.ds(384, 128)

    def copy_to(d):
        dx, dy, dz = d
        if dy == 0:
            slot = pl.ds(0, 4) if dx == 0 else pl.ds(0 if dx > 0 else 2, 2)
            layers = pl.ds(0, 4) if dx == 0 else pl.ds(2 if dx > 0 else 0, 2)
            if dz == 0:
                src, dst = own.at[:, layers], x_halo.at[:, slot]
            else:
                src = own.at[:, layers, :, lanes_of(dz > 0)]
                dst = z_halo.at[int(dx != 0), int(dz > 0), :, slot]
        else:
            src = strip_send.at[int(dy > 0)]
            if dz == 0:
                dst = pl.ds(128, 512)
            else:
                src = src.at[:, lanes_of(dz > 0)]
                dst = pl.ds(0 if dz > 0 else 640, 128)
            dst = strip_halo.at[dx + 1, int(dy > 0), :, dst]
        return remote(src, dst, AROUND.index(d), d), has(*d), has(-dx, -dy, -dz)

    def group(depth, strip):
        return [copy_to(d) for d in AROUND if (d[0] != 0) == depth and (d[1] != 0) == strip]

    x_copies, x_strips = group(True, False), group(True, True)
    a_copies, a_strips = group(False, False), group(False, True)

    def start(copies):
        for copy, send, _ in copies:
            pl.when(send)(copy.start)

    def wait_recv(copies):
        for copy, _, come in copies:
            pl.when(come)(copy.wait_recv)

    def wait_send(copies):
        for copy, send, _ in copies:
            pl.when(send)(copy.wait_send)

    arrivals = sum(has(*d).astype(jnp.int32) for d in AROUND)
    pl.semaphore_wait(barrier, arrivals)
    loads[0].wait()
    loads[1].wait()
    start(x_copies)
    start(a_copies)

    pack_strips(own, strip_send)
    start(x_strips)
    start(a_strips)

    for s in range(2):
        @pl.when(jnp.logical_not(has(STEP[s], 0, 0)))
        def _(s=s):
            x_halo[:, 2 * s : 2 * s + 2] = jnp.zeros((2, 2, 24, 512), BF16)
            for z in range(2):
                z_halo[1, z, :, 2 * s : 2 * s + 2] = jnp.zeros((2, 2, 24, 128), BF16)
                strip_halo[2 - 2 * s, z] = jnp.zeros((16, 768), BF16)

        @pl.when(jnp.logical_not(has(0, 0, -STEP[s])))
        def _(s=s):
            z_halo[0, s] = jnp.zeros((2, 4, 24, 128), BF16)
            for k in range(2):

                @pl.when(has(STEP[k], 0, 0))
                def _():
                    z_halo[1, s, :, 2 * k : 2 * k + 2] = jnp.zeros((2, 2, 24, 128), BF16)

        for z, (lane, size) in enumerate(((640, 128), (128, 512), (0, 128))):

            @pl.when(jnp.logical_not(has(0, -STEP[s], 1 - z)))
            def _(s=s, lane=lane, size=size):
                for side in range(3):
                    strip_halo[side, s, :, lane : lane + size] = jnp.zeros((16, size), BF16)

    loads[2].wait()
    band_store(bands.at[0], weights.at[0])

    loads[3].wait()
    band_store(bands.at[1], weights.at[1])

    wait_recv(a_copies)
    wait_recv(a_strips)
    assemble(grid, (2, 3, 4, 5), own, z_halo.at[0], (strip_halo.at[1],) * 4, range(4))

    loads[4].wait()
    loads[5].wait()
    bias_one = jnp.concatenate([biases[0]] * 4, axis=1)
    bias_two = jnp.concatenate([biases[1]] * 4, axis=1)

    def first_layer(begin, count):
        row = lax.broadcasted_iota(jnp.int32, (count, ROWS, 256), 1)
        lane = lax.broadcasted_iota(jnp.int32, (count, ROWS, 256), 2)
        layer = lax.broadcasted_iota(jnp.int32, (count, ROWS, 256), 0) + begin
        inside = (row < 24) | ((row == 24) & (iy < ny - 1)) | ((row == 31) & (iy > 0))
        inside &= (layer > 0) | (ix > 0)
        inside &= (layer < 5) | (ix < nx - 1)
        for block in range(3):
            size = 128 if block == 2 else 256
            conv = conv_narrow if block == 2 else conv_wide
            total = conv(grid, bands.at[0], begin, count, block * 256)
            value, slope = silu_pair(total, bias_one[:, :size])
            keep = inside[:, :, :size]
            if block == 0:
                keep &= (lane >= 64) | (iz > 0)
            if block == 2:
                keep &= (lane[:, :, :size] < 64) | (iz < nz - 1)
            for f, part in enumerate((value, slope)):
                hidden[f, begin : begin + count, :, block * 256 : block * 256 + size] = jnp.where(
                    keep, part, 0.0
                ).astype(BF16)

    first_layer(2, 2)

    wait_recv(x_copies)
    wait_recv(x_strips)
    assemble(grid, (0, 1, 6, 7), x_halo, z_halo.at[1], (strip_halo.at[2],) * 2 + (strip_halo.at[0],) * 2, (2, 3, 0, 1))
    first_layer(0, 2)
    first_layer(4, 2)

    for block in range(2):
        total = conv_wide(hidden, bands.at[1], 0, 4, block * 256)
        cols = pl.ds(block * 256, 256)
        out[:, :, cols] = total[0, :, 0:24] + bias_two
        out_tangent[:, :, cols] = total[1, :, 0:24]

    wait_send(x_copies)
    wait_send(a_copies)
    wait_send(a_strips)
    wait_send(x_strips)


def solution(mesh):
    nx, ny, nz = mesh.shape["gx"], mesh.shape["gy"], mesh.shape["gz"]

    def shards(source, tangent, w_one, b_one, w_two, b_two):
        assert source.shape == (4, 24, 512)
        hbm = pl.BlockSpec(memory_space=pltpu.HBM)
        vmem = pl.BlockSpec(memory_space=pltpu.VMEM)
        shape = pltpu.VMEM(source.shape, F32)
        pre, direction = pl.pallas_call(
            functools.partial(kernel, nx, ny, nz),
            out_shape=(shape, shape),
            in_specs=[hbm] * 6,
            out_specs=(vmem, vmem),
            scratch_shapes=[
                pltpu.VMEM((2, 4, 24, 512), BF16),
                pltpu.VMEM((2, 4, 24, 512), BF16),
                pltpu.VMEM((2, 2, 2, 4, 24, 128), BF16),
                pltpu.VMEM((2, 16, 512), BF16),
                pltpu.VMEM((3, 2, 16, 768), BF16),
                pltpu.VMEM((2, 3, 3, 3, 64, 64), BF16),
                pltpu.VMEM((2, 1, 64), F32),
                pltpu.VMEM((2, 1152, 768), BF16),
                pltpu.VMEM((2, 8, ROWS, 768), BF16),
                pltpu.VMEM((2, 6, ROWS, 640), BF16),
                pltpu.SemaphoreType.DMA((6,)),
                pltpu.SemaphoreType.DMA((len(AROUND),)),
                pltpu.SemaphoreType.DMA((len(AROUND),)),
            ],
            compiler_params=pltpu.CompilerParams(
                collective_id=0, has_side_effects=True, vmem_limit_bytes=62 * 1024 * 1024
            ),
        )(source, tangent, w_one, b_one.reshape(1, 64), w_two, b_two.reshape(1, 64))
        sig = jax.nn.sigmoid(pre)
        return (pre * sig).astype(BF16), (sig * (1.0 + pre * (1.0 - sig)) * direction).astype(BF16)
    return jax.shard_map(
        shards,
        mesh=mesh,
        in_specs=(P("gx", "gy", "gz"), P("gx", "gy", "gz"), P(), P(), P(), P()),
        out_specs=(P("gx", "gy", "gz"), P("gx", "gy", "gz")),
        check_vma=False,
    )
```

```python
import functools

import jax
import jax.numpy as jnp
from jax import lax
from jax.experimental import pallas as pl
from jax.experimental.pallas import tpu as pltpu
from jax.sharding import PartitionSpec as P

MESH = pl.DeviceIdType.MESH
F32 = jnp.float32
BF16 = jnp.bfloat16
ROWS = 32
AROUND = [
    (dx, dy, dz) for dx in (-1, 0, 1) for dy in (-1, 0, 1) for dz in (-1, 0, 1) if dx or dy or dz
]
STEP = (-1, 1)


def band_store(band, weight):
    zero64 = jnp.zeros((64, 64), BF16)
    zero128 = jnp.zeros((128, 128), BF16)
    for dx in range(3):
        for dy in range(3):
            taps = weight[dx, dy].reshape(192, 64)
            pair = jnp.concatenate(
                [
                    jnp.concatenate([taps, zero64], axis=0),
                    jnp.concatenate([zero64, taps], axis=0),
                ],
                axis=1,
            )
            r, c = dx * 384, dy * 256
            band[r : r + 256, c : c + 128] = pair
            band[r + 256 : r + 384, c : c + 128] = zero128
            band[r : r + 128, c + 128 : c + 256] = zero128
            band[r + 128 : r + 384, c + 128 : c + 256] = pair


def pack_strips(field, strips):
    row = lax.broadcasted_iota(jnp.int32, (8, 512), 0)
    low, high = [], []
    for f in range(2):
        first = jnp.zeros((8, 512), F32)
        last = jnp.zeros((8, 512), F32)
        for x in range(4):
            here = (row // 2) == x
            top = field[f, x, 0:8, :].astype(F32)
            end = field[f, x, 16:24, :].astype(F32)
            if x:
                top = pltpu.roll(top, 2 * x, 0)
            if x != 3:
                end = pltpu.roll(end, 2 + 2 * x, 0)
            first = jnp.where(here, top, first)
            last = jnp.where(here, end, last)
        low.append(first)
        high.append(last)
    strips[0] = jnp.concatenate(low, axis=0).astype(BF16)
    strips[1] = jnp.concatenate(high, axis=0).astype(BF16)


def assemble(grid, places, field, z_halo, strips, packed):
    row = lax.broadcasted_iota(jnp.int32, (8, 768), 0)
    for f in range(2):
        for x in range(4):
            place = places[x]
            grid[f, place, 0:24, 0:128] = z_halo[1, f, x]
            grid[f, place, 0:24, 128:640] = field[f, x]
            grid[f, place, 0:24, 640:768] = z_halo[0, f, x]
            at = packed[x]
            down = strips[x][0].astype(F32)[8 * f : 8 * f + 8]
            up = strips[x][1].astype(F32)[8 * f : 8 * f + 8]
            down = pltpu.roll(down, 8 - 2 * at, 0) if at else down
            up = pltpu.roll(up, 6 - 2 * at, 0) if at != 3 else up
            edge = jnp.where(row < 2, down, jnp.where(row >= 6, up, 0.0))
            grid[f, place, 24:32, :] = edge.astype(BF16)


def taps_sum(part, count, lanes):
    part = part.reshape(2 * count, ROWS, 3 * lanes)
    return (
        pltpu.roll(part[:, :, 0:lanes], 1, 1)
        + part[:, :, lanes : 2 * lanes]
        + pltpu.roll(part[:, :, 2 * lanes : 3 * lanes], ROWS - 1, 1)
    ).reshape(2, count, ROWS, lanes)


def conv_wide(grid, band, first, count, lane):
    rows = [
        grid[:, first + dx : first + dx + count, :, lane : lane + 384].reshape(
            2 * count * ROWS, 384
        )
        for dx in range(3)
    ]
    part = jnp.dot(
        jnp.concatenate(rows, axis=1), band[...], preferred_element_type=F32
    )
    return taps_sum(part, count, 256)


def conv_narrow(grid, band, first, count, lane):
    rows = [
        grid[:, first + dx : first + dx + count, :, lane : lane + 256].reshape(
            2 * count * ROWS, 256
        )
        for dx in range(3)
    ]
    weights = jnp.concatenate(
        [
            jnp.concatenate(
                [band[dx * 384 : dx * 384 + 256, dy * 256 : dy * 256 + 128] for dy in range(3)],
                axis=1,
            )
            for dx in range(3)
        ],
        axis=0,
    )
    part = jnp.dot(jnp.concatenate(rows, axis=1), weights, preferred_element_type=F32)
    return taps_sum(part, count, 128)


def silu_pair(total, bias):
    pre = total[0] + bias
    sig = jax.nn.sigmoid(pre)
    return pre * sig, sig * (1.0 + pre * (1.0 - sig)) * total[1]


def kernel(
    nx,
    ny,
    nz,
    source,
    tangent,
    w_one,
    b_one,
    w_two,
    b_two,
    out,
    out_tangent,
    own,
    x_halo,
    z_halo,
    strip_send,
    strip_halo,
    weights,
    biases,
    bands,
    grid,
    hidden,
    local_sem,
    send_sem,
    recv_sem,
):
    ix, iy, iz = lax.axis_index("gx"), lax.axis_index("gy"), lax.axis_index("gz")

    def has(dx, dy, dz):
        ok = None
        for i, n, d in ((ix, nx, dx), (iy, ny, dy), (iz, nz, dz)):
            if d:
                this = (i > 0) if d < 0 else (i < n - 1)
                ok = this if ok is None else ok & this
        return ok

    loads = [
        pltpu.make_async_copy(source, own.at[0], local_sem.at[0]),
        pltpu.make_async_copy(tangent, own.at[1], local_sem.at[1]),
        pltpu.make_async_copy(w_one, weights.at[0], local_sem.at[2]),
        pltpu.make_async_copy(w_two, weights.at[1], local_sem.at[3]),
        pltpu.make_async_copy(b_one, biases.at[0], local_sem.at[4]),
        pltpu.make_async_copy(b_two, biases.at[1], local_sem.at[5]),
    ]
    for load in loads:
        load.start()

    barrier = pltpu.get_barrier_semaphore()
    for d in AROUND:

        @pl.when(has(*d))
        def _(d=d):
            pl.semaphore_signal(
                barrier, inc=1, device_id=(ix + d[0], iy + d[1], iz + d[2]), device_id_type=MESH
            )

    def remote(src, dst, index, d):
        return pltpu.make_async_remote_copy(
            src_ref=src,
            dst_ref=dst,
            send_sem=send_sem.at[index],
            recv_sem=recv_sem.at[index],
            device_id=(ix + d[0], iy + d[1], iz + d[2]),
            device_id_type=MESH,
        )

    def lanes_of(s):
        return pl.ds(0, 128) if s == 0 else pl.ds(384, 128)

    def copy_to(d):
        dx, dy, dz = d
        if dy == 0:
            slot = pl.ds(0, 4) if dx == 0 else pl.ds(0 if dx > 0 else 2, 2)
            layers = pl.ds(0, 4) if dx == 0 else pl.ds(2 if dx > 0 else 0, 2)
            if dz == 0:
                src, dst = own.at[:, layers], x_halo.at[:, slot]
            else:
                src = own.at[:, layers, :, lanes_of(dz > 0)]
                dst = z_halo.at[int(dx != 0), int(dz > 0), :, slot]
        else:
            src = strip_send.at[int(dy > 0)]
            if dz == 0:
                dst = pl.ds(128, 512)
            else:
                src = src.at[:, lanes_of(dz > 0)]
                dst = pl.ds(0 if dz > 0 else 640, 128)
            dst = strip_halo.at[dx + 1, int(dy > 0), :, dst]
        return remote(src, dst, AROUND.index(d), d), has(*d), has(-dx, -dy, -dz)

    def group(depth, strip):
        return [copy_to(d) for d in AROUND if (d[0] != 0) == depth and (d[1] != 0) == strip]

    x_copies, x_strips = group(True, False), group(True, True)
    a_copies, a_strips = group(False, False), group(False, True)

    def start(copies):
        for copy, send, _ in copies:
            pl.when(send)(copy.start)

    def wait_recv(copies):
        for copy, _, come in copies:
            pl.when(come)(copy.wait_recv)

    def wait_send(copies):
        for copy, send, _ in copies:
            pl.when(send)(copy.wait_send)

    arrivals = sum(has(*d).astype(jnp.int32) for d in AROUND)
    pl.semaphore_wait(barrier, arrivals)
    loads[0].wait()
    loads[1].wait()
    start(x_copies)
    start(a_copies)

    pack_strips(own, strip_send)
    start(a_strips)
    start(x_strips)

    for s in range(2):
        @pl.when(jnp.logical_not(has(STEP[s], 0, 0)))
        def _(s=s):
            x_halo[:, 2 * s : 2 * s + 2] = jnp.zeros((2, 2, 24, 512), BF16)
            for z in range(2):
                z_halo[1, z, :, 2 * s : 2 * s + 2] = jnp.zeros((2, 2, 24, 128), BF16)
                strip_halo[2 - 2 * s, z] = jnp.zeros((16, 768), BF16)

        @pl.when(jnp.logical_not(has(0, 0, -STEP[s])))
        def _(s=s):
            z_halo[0, s] = jnp.zeros((2, 4, 24, 128), BF16)
            for k in range(2):

                @pl.when(has(STEP[k], 0, 0))
                def _():
                    z_halo[1, s, :, 2 * k : 2 * k + 2] = jnp.zeros((2, 2, 24, 128), BF16)

        for z, (lane, size) in enumerate(((640, 128), (128, 512), (0, 128))):

            @pl.when(jnp.logical_not(has(0, -STEP[s], 1 - z)))
            def _(s=s, lane=lane, size=size):
                for side in range(3):
                    strip_halo[side, s, :, lane : lane + size] = jnp.zeros((16, size), BF16)

    loads[2].wait()
    band_store(bands.at[0], weights.at[0])

    loads[3].wait()
    band_store(bands.at[1], weights.at[1])

    wait_recv(a_copies)
    wait_recv(a_strips)
    assemble(grid, (2, 3, 4, 5), own, z_halo.at[0], (strip_halo.at[1],) * 4, range(4))

    loads[4].wait()
    loads[5].wait()
    bias_one = jnp.concatenate([biases[0]] * 4, axis=1)
    bias_two = jnp.concatenate([biases[1]] * 4, axis=1)

    def first_layer(begin, count):
        row = lax.broadcasted_iota(jnp.int32, (count, ROWS, 256), 1)
        lane = lax.broadcasted_iota(jnp.int32, (count, ROWS, 256), 2)
        layer = lax.broadcasted_iota(jnp.int32, (count, ROWS, 256), 0) + begin
        inside = (row < 24) | ((row == 24) & (iy < ny - 1)) | ((row == 31) & (iy > 0))
        inside &= (layer > 0) | (ix > 0)
        inside &= (layer < 5) | (ix < nx - 1)
        for block in range(3):
            size = 128 if block == 2 else 256
            conv = conv_narrow if block == 2 else conv_wide
            total = conv(grid, bands.at[0], begin, count, block * 256)
            value, slope = silu_pair(total, bias_one[:, :size])
            keep = inside[:, :, :size]
            if block == 0:
                keep &= (lane >= 64) | (iz > 0)
            if block == 2:
                keep &= (lane[:, :, :size] < 64) | (iz < nz - 1)
            for f, part in enumerate((value, slope)):
                hidden[f, begin : begin + count, :, block * 256 : block * 256 + size] = jnp.where(
                    keep, part, 0.0
                ).astype(BF16)

    first_layer(2, 2)

    wait_recv(x_copies)
    wait_recv(x_strips)
    assemble(grid, (0, 1, 6, 7), x_halo, z_halo.at[1], (strip_halo.at[2],) * 2 + (strip_halo.at[0],) * 2, (2, 3, 0, 1))
    first_layer(0, 2)
    first_layer(4, 2)

    for block in range(2):
        total = conv_wide(hidden, bands.at[1], 0, 4, block * 256)
        cols = pl.ds(block * 256, 256)
        out[:, :, cols] = total[0, :, 0:24] + bias_two
        out_tangent[:, :, cols] = total[1, :, 0:24]

    wait_send(x_copies)
    wait_send(a_copies)
    wait_send(a_strips)
    wait_send(x_strips)


def solution(mesh):
    nx, ny, nz = mesh.shape["gx"], mesh.shape["gy"], mesh.shape["gz"]

    def shards(source, tangent, w_one, b_one, w_two, b_two):
        assert source.shape == (4, 24, 512)
        hbm = pl.BlockSpec(memory_space=pltpu.HBM)
        vmem = pl.BlockSpec(memory_space=pltpu.VMEM)
        shape = pltpu.VMEM(source.shape, F32)
        pre, direction = pl.pallas_call(
            functools.partial(kernel, nx, ny, nz),
            out_shape=(shape, shape),
            in_specs=[hbm] * 6,
            out_specs=(vmem, vmem),
            scratch_shapes=[
                pltpu.VMEM((2, 4, 24, 512), BF16),
                pltpu.VMEM((2, 4, 24, 512), BF16),
                pltpu.VMEM((2, 2, 2, 4, 24, 128), BF16),
                pltpu.VMEM((2, 16, 512), BF16),
                pltpu.VMEM((3, 2, 16, 768), BF16),
                pltpu.VMEM((2, 3, 3, 3, 64, 64), BF16),
                pltpu.VMEM((2, 1, 64), F32),
                pltpu.VMEM((2, 1152, 768), BF16),
                pltpu.VMEM((2, 8, ROWS, 768), BF16),
                pltpu.VMEM((2, 6, ROWS, 640), BF16),
                pltpu.SemaphoreType.DMA((6,)),
                pltpu.SemaphoreType.DMA((len(AROUND),)),
                pltpu.SemaphoreType.DMA((len(AROUND),)),
            ],
            compiler_params=pltpu.CompilerParams(
                collective_id=0, has_side_effects=True, vmem_limit_bytes=62 * 1024 * 1024
            ),
        )(source, tangent, w_one, b_one.reshape(1, 64), w_two, b_two.reshape(1, 64))
        sig = jax.nn.sigmoid(pre)
        return (pre * sig).astype(BF16), (sig * (1.0 + pre * (1.0 - sig)) * direction).astype(BF16)
    return jax.shard_map(
        shards,
        mesh=mesh,
        in_specs=(P("gx", "gy", "gz"), P("gx", "gy", "gz"), P(), P(), P(), P()),
        out_specs=(P("gx", "gy", "gz"), P("gx", "gy", "gz")),
        check_vma=False,
    )
```
